32 devices in a mesh: gz: 8 (over z, core), gy: 4 (over y, x).
Axes of the slice: x: 2, y: 2, z: 4, core: 2. Of those that a mesh axis runs over, the one named last changes fastest.
Arguments:
- tokens: bfloat16 [1, 16, 8, 64, 512], P(None, 'gz', 'gy'), may hold values from -75 to 75
- w_qkv: bfloat16 [512, 1536], replicated, may hold values from -0.25 to 0.25
- w_out: bfloat16 [512, 512], replicated, may hold values from -0.25 to 0.25
- rel_bias: float32 [16, 5, 5, 5], replicated, may hold values from -4 to 4
- gain: float32 [512], replicated, may hold values from 0.5 to 1.5
Outputs:
- update: bfloat16 [1, 16, 8, 64, 512], P(None, 'gz', 'gy')
The draws below stay inside these ranges and needn't reach their ends.
All inputs are finite; a program needn't handle non-finite values.
Results may differ from the reference program's by a relative error of at most 0.0079.
Values may be sent and summed in bfloat16 or wider, within the bound.
A program may use at most 128 MiB of HBM per device.

```python
import jax
import jax.numpy as jnp
from jax import lax

D = 512
H = 16
HD = 32
KERNEL = 5
DILATION_DEPTH = 8
XLEN = 64
BOX = 1
DEPTH_TOKENS = 16
YLEN = 8


def draw_tokens(key, part):
    full_shape = (BOX, DEPTH_TOKENS, YLEN, XLEN, D)
    key_base = jax.random.fold_in(key, 0)
    result = jnp.clip(jax.random.normal(key_base, full_shape, jnp.float32), -6.0, 6.0)
    return result.astype(jnp.bfloat16)


def bell_draw(stream_key, dims, scale, limit, held_as=jnp.bfloat16):
    return jnp.clip(scale * jax.random.normal(stream_key, dims, jnp.float32), -limit, limit).astype(held_as)


def setup_inputs(seed: int = 0) -> dict:
    streams_of = jax.random.split(jax.random.key(seed), 6)
    return {
        "tokens": draw_tokens(jax.random.fold_in(streams_of[5], 71), 0),
        "w_qkv": bell_draw(streams_of[1], (D, 3 * D), D ** -0.5, 0.25),
        "w_out": bell_draw(streams_of[2], (D, D), D ** -0.5, 0.25),
        "rel_bias": bell_draw(streams_of[3], (H, KERNEL, KERNEL, KERNEL), 1.0, 4.0, jnp.float32),
        "gain": jnp.clip(1.0 + 0.1 * jax.random.normal(streams_of[4], (D,), jnp.float32), 0.5, 1.5),
    }


def reference(tokens, w_qkv, w_out, rel_bias, gain):
    kernel_radius = KERNEL // 2
    flat_tokens = tokens.reshape(-1, D)
    projected = jnp.dot(flat_tokens, w_qkv, preferred_element_type=jnp.float32).astype(jnp.bfloat16)
    projected = projected.reshape(BOX, DEPTH_TOKENS, YLEN, XLEN, H, 3, HD)
    score_scale = float(HD) ** (-0.5)

    def one_plane(depth_plane_index):
        own_plane = lax.dynamic_index_in_dim(projected, depth_plane_index, 1, keepdims=False)
        queries = own_plane[..., 0, :].astype(jnp.float32)
        scores = []
        for depth_tap in range(KERNEL):
            source_plane = (depth_plane_index + DILATION_DEPTH * (depth_tap - kernel_radius)) % DEPTH_TOKENS
            key_plane = lax.dynamic_index_in_dim(projected, source_plane, 1, keepdims=False)
            for tap_y in range(KERNEL):
                for tap_x in range(KERNEL):
                    shifted = jnp.roll(key_plane, (kernel_radius - tap_y, kernel_radius - tap_x), axis=(1, 2))
                    dotted = lax.optimization_barrier(jnp.sum(queries * shifted[..., 1, :].astype(jnp.float32), axis=-1))
                    scores.append(dotted * score_scale + rel_bias[:, depth_tap, tap_y, tap_x])
        stacked = jnp.stack(scores, -1)
        row_max = lax.optimization_barrier(jnp.max(stacked, axis=-1, keepdims=True))
        exponent = jnp.exp(stacked - row_max)
        weights = (exponent / lax.optimization_barrier(jnp.sum(exponent, axis=-1, keepdims=True))).astype(jnp.bfloat16)
        summed = jnp.zeros(queries.shape, jnp.float32)
        position = 0
        for depth_tap in range(KERNEL):
            source_plane = (depth_plane_index + DILATION_DEPTH * (depth_tap - kernel_radius)) % DEPTH_TOKENS
            key_plane = lax.dynamic_index_in_dim(projected, source_plane, 1, keepdims=False)
            for tap_y in range(KERNEL):
                for tap_x in range(KERNEL):
                    shifted = jnp.roll(key_plane, (kernel_radius - tap_y, kernel_radius - tap_x), axis=(1, 2))
                    summed = summed + weights[..., position, None].astype(jnp.float32) * shifted[..., 2, :].astype(jnp.float32)
                    position = position + 1
        return summed.astype(jnp.bfloat16).reshape(BOX, YLEN, XLEN, D)
    per_plane = lax.map(one_plane, jnp.arange(DEPTH_TOKENS, dtype=jnp.int32))
    attended = jnp.moveaxis(per_plane, 0, 1)
    projection = jnp.dot(attended.reshape(-1, D), w_out, preferred_element_type=jnp.float32)
    mean_sq = lax.optimization_barrier(jnp.mean(projection * projection, axis=-1, keepdims=True))
    update = projection * lax.rsqrt(mean_sq + 1e-06) * gain
    return update.astype(jnp.bfloat16).reshape(BOX, DEPTH_TOKENS, YLEN, XLEN, D)
```

```python
import functools

import jax
import jax.numpy as jnp
from jax import lax
from jax.experimental import pallas as pl
from jax.experimental.pallas import tpu as pltpu
from jax.sharding import PartitionSpec as P

DILATION_DEPTH = 8


def shifted(block, axis, distance):
    devices = range(lax.axis_size(axis))
    route = [((i - distance) % len(devices), i) for i in devices]
    return lax.ppermute(block, axis, route)


def pick_rows(y_rows, per_row):
    chosen = 1
    for candidate in range(1, y_rows + 1):
        if y_rows % candidate == 0 and candidate * per_row <= 1024:
            chosen = candidate
    return chosen


def collect_planes(key_value, depth_stride, kernel_radius):
    axis_count = lax.axis_size("gz")
    received = {0: key_value}
    for offset in range(-kernel_radius, kernel_radius + 1):
        if offset != 0:
            distance = -offset * depth_stride % axis_count
            if distance == 0:
                received[offset] = key_value
            else:
                received[offset] = shifted(key_value, "gz", distance)
    return jnp.stack([received[offset] for offset in range(-kernel_radius, kernel_radius + 1)], 0)


def neighbourhood(queries, padded, bias_part):
    boxes, depth_planes, y_rows, x_cells, local_heads, head_dim = queries.shape
    kernel = padded.shape[0]
    kernel_radius = kernel // 2
    score_scale = float(head_dim) ** (-0.5)
    block_rows = pick_rows(y_rows, local_heads * x_cells)
    row_blocks = y_rows // block_rows
    block_count = boxes * depth_planes * row_blocks

    def tap_window(wide, tap_y):
        rows_part = wide[:, tap_y : tap_y + block_rows]
        return jnp.stack([rows_part[:, :, tap_x : tap_x + x_cells] for tap_x in range(kernel)], 1)

    def one_block(block_index):
        slab_index = block_index // row_blocks
        row_start = block_index % row_blocks * block_rows
        box_index = slab_index // depth_planes
        depth_plane_index = slab_index % depth_planes
        query_block = lax.dynamic_slice(
            queries,
            (box_index, depth_plane_index, row_start, 0, 0, 0),
            (1, 1, block_rows, x_cells, local_heads, head_dim),
        )[0, 0]
        pair_block = lax.dynamic_slice(
            padded,
            (0, box_index, depth_plane_index, row_start, 0, 0, 0, 0),
            (kernel, 1, 1, block_rows + 2 * kernel_radius, x_cells, local_heads, 2, head_dim),
        )[:, 0, 0]
        wide = jnp.concatenate(
            [
                pair_block[:, :, x_cells - kernel_radius :],
                pair_block,
                pair_block[:, :, :kernel_radius],
            ],
            axis=2,
        )
        score_parts = []
        for tap_y in range(kernel):
            window = tap_window(wide, tap_y)
            score_parts.append(
                jnp.einsum(
                    "yxhd,abyxhd->yhxab",
                    query_block,
                    window[..., 0, :],
                    preferred_element_type=jnp.float32,
                )
            )
        scores = jnp.stack(score_parts, 4) * score_scale + bias_part[None, :, None]
        row_max = jnp.max(scores, axis=(3, 4, 5), keepdims=True)
        exponent = jnp.exp(scores - row_max)
        weights = (exponent / jnp.sum(exponent, axis=(3, 4, 5), keepdims=True)).astype(jnp.bfloat16)
        mixed = jnp.zeros((block_rows, x_cells, local_heads, head_dim), jnp.float32)
        for tap_y in range(kernel):
            window = tap_window(wide, tap_y)
            mixed = mixed + jnp.einsum(
                "yhxab,abyxhd->yxhd",
                weights[:, :, :, :, tap_y],
                window[..., 1, :],
                preferred_element_type=jnp.float32,
            )
        return mixed.astype(jnp.bfloat16).reshape(block_rows, x_cells, local_heads * head_dim)

    block_out = lax.map(one_block, jnp.arange(block_count, dtype=jnp.int32))
    return block_out.reshape(boxes, depth_planes, y_rows, x_cells, local_heads * head_dim)


def body(tokens, w_qkv, w_out, rel_bias, gain):
    boxes, depth_planes, y_rows, x_cells, model_width = tokens.shape
    head_count = rel_bias.shape[0]
    kernel = rel_bias.shape[1]
    kernel_radius = kernel // 2
    head_dim = model_width // head_count
    depth_stride = DILATION_DEPTH // depth_planes
    projected = jnp.dot(
        tokens.reshape(-1, model_width), w_qkv, preferred_element_type=jnp.float32
    ).astype(jnp.bfloat16)
    projected = projected.reshape(boxes, depth_planes, y_rows, x_cells, 3 * model_width)
    exchanged = lax.all_to_all(projected, "gy", split_axis=4, concat_axis=2, tiled=True)
    local_heads = exchanged.shape[-1] // (3 * head_dim)
    unpacked = exchanged.reshape(exchanged.shape[:4] + (local_heads, 3, head_dim))
    queries = unpacked[..., 0, :]
    key_value = unpacked[..., 1:, :]
    plane_taps = collect_planes(key_value, depth_stride, kernel_radius)
    padded = jnp.concatenate(
        [plane_taps[:, :, :, -kernel_radius:], plane_taps, plane_taps[:, :, :, :kernel_radius]],
        axis=3,
    )
    head_start = lax.axis_index("gy") * local_heads
    bias_part = lax.dynamic_slice_in_dim(rel_bias, head_start, local_heads, 0)
    gathered = neighbourhood(queries, padded, bias_part)
    attended = lax.all_to_all(gathered, "gy", split_axis=2, concat_axis=4, tiled=True)
    projection = jnp.dot(
        attended.reshape(-1, model_width), w_out, preferred_element_type=jnp.float32
    )
    mean_sq = jnp.mean(projection * projection, axis=-1, keepdims=True)
    update = (projection * lax.rsqrt(mean_sq + 1e-06) * gain).astype(jnp.bfloat16)
    return update.reshape(boxes, depth_planes, y_rows, x_cells, model_width)


MASKED = -1e30
LOG2E = 1.4426950408889634
MESH_IDS = pl.DeviceIdType.MESH


def kernel_body(
    members, ring, half, tap_groups, radius, scale,
    tok_ref, wqkv_ref, wout_ref, bias_ref, gain_ref, out_ref,
    wqkv, wout, regrouped, halo_out, main_in, halo_in, bias_full, qkv, attended, returned,
    weight_sems, main_send, main_recv, halo_send, halo_recv, back_send, back_recv, local_sem,
):
    heads, kernel = bias_ref.shape[0], bias_ref.shape[2]
    rows, x_cells, width = tok_ref.shape[2:]
    chunk = x_cells // ring
    y_total = rows * ring
    head_dim = width // heads
    lanes = y_total * chunk
    groups = width // lanes
    per_group = lanes // head_dim
    halo_rows = halo_in.shape[1]
    halo_slots = halo_rows // rows
    keys = members * lanes + members * ring * halo_rows
    gz, gy = lax.axis_index("gz"), lax.axis_index("gy")
    mine, base = gz // half, gz % half
    slot = mine * ring + gy
    partners = [(dm, dg) for dm in reversed(range(members)) for dg in range(ring) if (dm, dg) != (0, 0)]

    def member(dm):
        return lax.rem(mine + dm, members)

    def ring_place(dg):
        return lax.rem(gy + dg, ring)

    def target(dm, dg):
        return (base + member(dm) * half, ring_place(dg))

    barrier = pltpu.get_barrier_semaphore()
    for dm, dg in partners:
        pl.semaphore_signal(barrier, inc=1, device_id=target(dm, dg), device_id_type=MESH_IDS)
    load_qkv = pltpu.make_async_copy(wqkv_ref, wqkv, weight_sems.at[0])
    load_out = pltpu.make_async_copy(wout_ref, wout, weight_sems.at[1])
    load_qkv.start()
    load_out.start()

    count = ring * halo_rows
    line = lax.broadcasted_iota(jnp.int32, (count, rows * x_cells), 0)
    source = lax.broadcasted_iota(jnp.int32, (count, rows * x_cells), 1)
    place, within = line // halo_rows, line % halo_rows
    row, column = within // halo_slots, within % halo_slots
    column_x = place * chunk + jnp.where(column < radius, column - radius, column + chunk - radius)
    wanted = row * x_cells + (column_x + x_cells) % x_cells
    pick = jnp.where((source == wanted) & (column < 2 * radius), 1.0, 0.0).astype(jnp.bfloat16)
    for plane in range(members):
        flat = tok_ref[0, plane].reshape(rows * x_cells, width)
        picked = jnp.dot(pick, flat, preferred_element_type=jnp.float32).astype(jnp.bfloat16)
        halo_out[plane] = picked.reshape(ring, halo_rows, width)

    pl.semaphore_wait(barrier, len(partners))
    sends = []
    for dm, dg in partners:
        index = dm * ring + dg
        columns = pl.ds(pl.multiple_of(ring_place(dg) * chunk, chunk), chunk)
        sends.append(
            pltpu.make_async_remote_copy(
                src_ref=tok_ref.at[0, member(dm), :, columns, :],
                dst_ref=main_in.at[slot],
                send_sem=main_send.at[index],
                recv_sem=main_recv.at[index],
                device_id=target(dm, dg),
                device_id_type=MESH_IDS,
            )
        )
        sends.append(
            pltpu.make_async_remote_copy(
                src_ref=halo_out.at[member(dm), ring_place(dg)],
                dst_ref=halo_in.at[slot],
                send_sem=halo_send.at[index],
                recv_sem=halo_recv.at[index],
                device_id=target(dm, dg),
                device_id_type=MESH_IDS,
            )
        )
    for copy in sends:
        copy.start()
    own_columns = pl.ds(pl.multiple_of(gy * chunk, chunk), chunk)
    main_in[slot] = tok_ref[0, mine, :, own_columns, :]
    halo_in[slot] = halo_out[mine, gy]

    x_query = lax.broadcasted_iota(jnp.int32, (chunk, lanes), 0)
    lane = lax.broadcasted_iota(jnp.int32, (chunk, lanes), 1)

    def tap_map(y_key, x_key, valid):
        tap_y = (y_key + radius) % y_total
        tap_x = x_key - x_query + radius
        inside = valid & (tap_y < kernel) & (tap_x >= 0) & (tap_x < kernel)
        return jnp.where(inside, tap_y * kernel + tap_x, -1)

    main_taps = tap_map(lane // chunk, lane % chunk, lane >= 0)
    halo_lane = lane % (y_total * halo_slots)
    halo_column = halo_lane % halo_slots
    halo_x = jnp.where(halo_column < radius, halo_column - radius, halo_column + chunk - radius)
    halo_taps = tap_map(halo_lane // halo_slots, halo_x, halo_column < 2 * radius)
    first_half = lane < y_total * halo_slots

    def bias_of_head(head, carry):
        mains, halos = [], []
        for taps in tap_groups:
            parts = [bias_ref[head, i] for i in taps]
            top = functools.reduce(jnp.maximum, parts)
            merged = (top + jnp.log(sum(jnp.exp(part - top) for part in parts))) * LOG2E
            main = jnp.full((chunk, lanes), MASKED, jnp.float32)
            halo = main
            for tap_x in range(kernel):
                spread = jnp.broadcast_to(merged[:, tap_x : tap_x + 1], (kernel, lanes))
                for tap_y in range(kernel):
                    value = spread[tap_y : tap_y + 1, :]
                    main = jnp.where(main_taps == tap_y * kernel + tap_x, value, main)
                    halo = jnp.where(halo_taps == tap_y * kernel + tap_x, value, halo)
            mains.append(main)
            halos.append(halo)
        for y in range(y_total):
            here = pl.ds(y * chunk, chunk)
            turned = [pltpu.roll(main, y * chunk, 1) if y else main for main in mains]
            turned_halo = [pltpu.roll(halo, y * halo_slots, 1) if y else halo for halo in halos]
            for plane in range(2):
                bias_full[head, plane, here, 0:lanes] = turned[plane]
                bias_full[head, plane, here, lanes : 2 * lanes] = turned[1 - plane]
                bias_full[head, plane, here, 2 * lanes : 3 * lanes] = jnp.where(
                    first_half, turned_halo[plane], turned_halo[1 - plane]
                )
        return carry

    lax.fori_loop(0, heads, bias_of_head, 0)

    span = 3 * lanes
    before = lax.broadcasted_iota(jnp.int32, (span, span), 0)
    after = lax.broadcasted_iota(jnp.int32, (span, span), 1)
    origin = (after % lanes) // head_dim * (3 * head_dim) + after // lanes * head_dim + after % head_dim
    order = jnp.where(before == origin, 1.0, 0.0).astype(jnp.bfloat16)
    load_qkv.wait()
    for group in range(groups):
        regrouped[group] = jnp.dot(
            wqkv[:, group * span : (group + 1) * span], order, preferred_element_type=jnp.float32
        ).astype(jnp.bfloat16)

    for copy in sends:
        copy.wait_recv()
    main = main_in[...].reshape(members * lanes, width)
    halo = halo_in[...].reshape(members * ring * halo_rows, width)
    for group in range(groups):
        weight = regrouped[group]
        qkv[group, 0 : members * lanes] = jnp.dot(
            main, weight, preferred_element_type=jnp.float32
        ).astype(jnp.bfloat16)
        qkv[group, members * lanes : keys] = jnp.dot(
            halo, weight, preferred_element_type=jnp.float32
        ).astype(jnp.bfloat16)

    owner = lax.broadcasted_iota(jnp.int32, (lanes, lanes), 1) // head_dim
    ones = jnp.ones((keys, lanes), jnp.bfloat16)
    load_out.wait()
    backs = []
    for dm in reversed(range(members)):
        plane = member(dm)
        query_rows = pl.ds(pl.multiple_of(plane * lanes, lanes), lanes)

        def attend(group, carry):
            query = qkv[group, query_rows, 0:lanes]
            key = qkv[group, :, lanes : 2 * lanes]
            value = jnp.concatenate([qkv[group, :, 2 * lanes : 3 * lanes], ones], axis=1)
            mixed = jnp.zeros((lanes, lanes), jnp.float32)
            for within in range(per_group):
                own = jnp.where(owner == within, query, jnp.zeros_like(query))
                scores = lax.dot_general(
                    own, key, (((1,), (1,)), ((), ())), preferred_element_type=jnp.float32
                )
                scores = scores * (scale * LOG2E) + bias_full[group * per_group + within, plane]
                row_max = jnp.max(scores, axis=1, keepdims=True)
                weights = jnp.exp2(scores - row_max).astype(jnp.bfloat16)
                both = jnp.dot(weights, value, preferred_element_type=jnp.float32)
                mixed = jnp.where(owner == within, both[:, :lanes] / both[:, lanes:], mixed)
            attended[group] = mixed.astype(jnp.bfloat16)
            return carry

        lax.fori_loop(0, groups, attend, 0)
        joined = jnp.concatenate([attended[group] for group in range(groups)], axis=1)
        projection = jnp.dot(joined, wout[...], preferred_element_type=jnp.float32)
        mean_sq = jnp.mean(projection * projection, axis=-1, keepdims=True)
        update = (projection * lax.rsqrt(mean_sq + 1e-06) * gain_ref[...]).astype(jnp.bfloat16)
        returned[dm] = update.reshape(ring, rows, chunk, width)
        for dg in range(ring):
            index = dm * ring + dg
            landing = out_ref.at[0, mine, :, own_columns, :]
            if (dm, dg) == (0, 0):
                own_copy = pltpu.make_async_copy(returned.at[dm, gy], landing, local_sem)
                own_copy.start()
            else:
                back = pltpu.make_async_remote_copy(
                    src_ref=returned.at[dm, ring_place(dg)],
                    dst_ref=landing,
                    send_sem=back_send.at[index],
                    recv_sem=back_recv.at[index],
                    device_id=target(dm, dg),
                    device_id_type=MESH_IDS,
                )
                back.start()
                backs.append(back)
    for copy in sends:
        copy.wait_send()
    for copy in backs:
        copy.wait()
    own_copy.wait()


def pair_plan(mesh_shape, depth_total, shapes):
    boxes, planes, rows, x_cells, width, heads, kernel = shapes
    depth_devices, ring = mesh_shape
    radius = kernel // 2
    head_dim = width // heads
    offsets = [DILATION_DEPTH * (i - radius) % depth_total for i in range(kernel)]
    halo_slots = 8
    if boxes != 1 or planes != 2 or depth_total != 2 * DILATION_DEPTH or depth_devices % 2:
        return None
    if x_cells % ring or kernel % 2 == 0:
        return None
    chunk, y_total = x_cells // ring, rows * ring
    lanes = chunk * y_total
    if lanes != 128 or chunk % 16 or kernel > y_total or 2 * y_total * halo_slots != lanes:
        return None
    if rows * halo_slots % 16 or 2 * radius > halo_slots or lanes % head_dim or width % lanes:
        return None
    return halo_slots, [[i for i in range(kernel) if offsets[i] == p * DILATION_DEPTH] for p in range(2)]


def fused(plan, depth_devices, ring, tokens, w_qkv, w_out, rel_bias, gain):
    halo_slots, tap_groups = plan
    _, planes, rows, x_cells, width = tokens.shape
    heads, kernel = rel_bias.shape[0], rel_bias.shape[1]
    chunk = x_cells // ring
    lanes = chunk * rows * ring
    groups = width // lanes
    halo_rows = rows * halo_slots
    members, slots = planes, planes * ring
    keys = 3 * lanes
    vmem = pl.BlockSpec(memory_space=pltpu.VMEM)
    anywhere = pl.BlockSpec(memory_space=pl.ANY)
    body_of = functools.partial(
        kernel_body, members, ring, depth_devices // 2, tap_groups, kernel // 2,
        float(width // heads) ** (-0.5),
    )
    dma = pltpu.SemaphoreType.DMA
    return pl.pallas_call(
        body_of,
        out_shape=jax.ShapeDtypeStruct(tokens.shape, jnp.bfloat16),
        in_specs=[vmem, anywhere, anywhere, vmem, vmem],
        out_specs=anywhere,
        scratch_shapes=[
            pltpu.VMEM(w_qkv.shape, jnp.bfloat16),
            pltpu.VMEM(w_out.shape, jnp.bfloat16),
            pltpu.VMEM((groups, width, 3 * lanes), jnp.bfloat16),
            pltpu.VMEM((members, ring, halo_rows, width), jnp.bfloat16),
            pltpu.VMEM((slots, rows, chunk, width), jnp.bfloat16),
            pltpu.VMEM((slots, halo_rows, width), jnp.bfloat16),
            pltpu.VMEM((heads, members, lanes, keys), jnp.float32),
            pltpu.VMEM((groups, keys, 3 * lanes), jnp.bfloat16),
            pltpu.VMEM((groups, lanes, lanes), jnp.bfloat16),
            pltpu.VMEM((members, ring, rows, chunk, width), jnp.bfloat16),
            dma((2,)), dma((slots,)), dma((slots,)), dma((slots,)), dma((slots,)),
            dma((slots,)), dma((slots,)), dma,
        ],
        compiler_params=pltpu.CompilerParams(
            collective_id=0, has_side_effects=True, vmem_limit_bytes=40 * 1024 * 1024
        ),
    )(tokens, w_qkv, w_out, rel_bias, gain.reshape(1, width))


def solution(mesh):
    depth_devices, ring = mesh.shape["gz"], mesh.shape["gy"]

    def chosen(tokens, w_qkv, w_out, rel_bias, gain):
        shapes = tokens.shape + rel_bias.shape[:2]
        plan = pair_plan((depth_devices, ring), tokens.shape[1] * depth_devices, shapes)
        if plan is None:
            return body(tokens, w_qkv, w_out, rel_bias, gain)
        return fused(plan, depth_devices, ring, tokens, w_qkv, w_out, rel_bias, gain)

    in_specs = (P(None, "gz", "gy", None, None), P(), P(), P(), P())
    out_specs = P(None, "gz", "gy", None, None)
    return jax.shard_map(chosen, mesh=mesh, in_specs=in_specs, out_specs=out_specs, check_vma=False)
```

```python
import functools

import jax
import jax.numpy as jnp
from jax import lax
from jax.experimental import pallas as pl
from jax.experimental.pallas import tpu as pltpu
from jax.sharding import PartitionSpec as P

DILATION_DEPTH = 8


def shifted(block, axis, distance):
    devices = range(lax.axis_size(axis))
    route = [((i - distance) % len(devices), i) for i in devices]
    return lax.ppermute(block, axis, route)


def pick_rows(y_rows, per_row):
    chosen = 1
    for candidate in range(1, y_rows + 1):
        if y_rows % candidate == 0 and candidate * per_row <= 1024:
            chosen = candidate
    return chosen


def collect_planes(key_value, depth_stride, kernel_radius):
    axis_count = lax.axis_size("gz")
    received = {0: key_value}
    for offset in range(-kernel_radius, kernel_radius + 1):
        if offset != 0:
            distance = -offset * depth_stride % axis_count
            if distance == 0:
                received[offset] = key_value
            else:
                received[offset] = shifted(key_value, "gz", distance)
    return jnp.stack([received[offset] for offset in range(-kernel_radius, kernel_radius + 1)], 0)


def neighbourhood(queries, padded, bias_part):
    boxes, depth_planes, y_rows, x_cells, local_heads, head_dim = queries.shape
    kernel = padded.shape[0]
    kernel_radius = kernel // 2
    score_scale = float(head_dim) ** (-0.5)
    block_rows = pick_rows(y_rows, local_heads * x_cells)
    row_blocks = y_rows // block_rows
    block_count = boxes * depth_planes * row_blocks

    def tap_window(wide, tap_y):
        rows_part = wide[:, tap_y : tap_y + block_rows]
        return jnp.stack([rows_part[:, :, tap_x : tap_x + x_cells] for tap_x in range(kernel)], 1)

    def one_block(block_index):
        slab_index = block_index // row_blocks
        row_start = block_index % row_blocks * block_rows
        box_index = slab_index // depth_planes
        depth_plane_index = slab_index % depth_planes
        query_block = lax.dynamic_slice(
            queries,
            (box_index, depth_plane_index, row_start, 0, 0, 0),
            (1, 1, block_rows, x_cells, local_heads, head_dim),
        )[0, 0]
        pair_block = lax.dynamic_slice(
            padded,
            (0, box_index, depth_plane_index, row_start, 0, 0, 0, 0),
            (kernel, 1, 1, block_rows + 2 * kernel_radius, x_cells, local_heads, 2, head_dim),
        )[:, 0, 0]
        wide = jnp.concatenate(
            [
                pair_block[:, :, x_cells - kernel_radius :],
                pair_block,
                pair_block[:, :, :kernel_radius],
            ],
            axis=2,
        )
        score_parts = []
        for tap_y in range(kernel):
            window = tap_window(wide, tap_y)
            score_parts.append(
                jnp.einsum(
                    "yxhd,abyxhd->yhxab",
                    query_block,
                    window[..., 0, :],
                    preferred_element_type=jnp.float32,
                )
            )
        scores = jnp.stack(score_parts, 4) * score_scale + bias_part[None, :, None]
        row_max = jnp.max(scores, axis=(3, 4, 5), keepdims=True)
        exponent = jnp.exp(scores - row_max)
        weights = (exponent / jnp.sum(exponent, axis=(3, 4, 5), keepdims=True)).astype(jnp.bfloat16)
        mixed = jnp.zeros((block_rows, x_cells, local_heads, head_dim), jnp.float32)
        for tap_y in range(kernel):
            window = tap_window(wide, tap_y)
            mixed = mixed + jnp.einsum(
                "yhxab,abyxhd->yxhd",
                weights[:, :, :, :, tap_y],
                window[..., 1, :],
                preferred_element_type=jnp.float32,
            )
        return mixed.astype(jnp.bfloat16).reshape(block_rows, x_cells, local_heads * head_dim)

    block_out = lax.map(one_block, jnp.arange(block_count, dtype=jnp.int32))
    return block_out.reshape(boxes, depth_planes, y_rows, x_cells, local_heads * head_dim)


def body(tokens, w_qkv, w_out, rel_bias, gain):
    boxes, depth_planes, y_rows, x_cells, model_width = tokens.shape
    head_count = rel_bias.shape[0]
    kernel = rel_bias.shape[1]
    kernel_radius = kernel // 2
    head_dim = model_width // head_count
    depth_stride = DILATION_DEPTH // depth_planes
    projected = jnp.dot(
        tokens.reshape(-1, model_width), w_qkv, preferred_element_type=jnp.float32
    ).astype(jnp.bfloat16)
    projected = projected.reshape(boxes, depth_planes, y_rows, x_cells, 3 * model_width)
    exchanged = lax.all_to_all(projected, "gy", split_axis=4, concat_axis=2, tiled=True)
    local_heads = exchanged.shape[-1] // (3 * head_dim)
    unpacked = exchanged.reshape(exchanged.shape[:4] + (local_heads, 3, head_dim))
    queries = unpacked[..., 0, :]
    key_value = unpacked[..., 1:, :]
    plane_taps = collect_planes(key_value, depth_stride, kernel_radius)
    padded = jnp.concatenate(
        [plane_taps[:, :, :, -kernel_radius:], plane_taps, plane_taps[:, :, :, :kernel_radius]],
        axis=3,
    )
    head_start = lax.axis_index("gy") * local_heads
    bias_part = lax.dynamic_slice_in_dim(rel_bias, head_start, local_heads, 0)
    gathered = neighbourhood(queries, padded, bias_part)
    attended = lax.all_to_all(gathered, "gy", split_axis=2, concat_axis=4, tiled=True)
    projection = jnp.dot(
        attended.reshape(-1, model_width), w_out, preferred_element_type=jnp.float32
    )
    mean_sq = jnp.mean(projection * projection, axis=-1, keepdims=True)
    update = (projection * lax.rsqrt(mean_sq + 1e-06) * gain).astype(jnp.bfloat16)
    return update.reshape(boxes, depth_planes, y_rows, x_cells, model_width)


SPLITS = 1
MASKED = -1e30
LOG2E = 1.4426950408889634
MESH_IDS = pl.DeviceIdType.MESH


def kernel_body(
    members, ring, half, tap_groups, radius, scale,
    tok_hbm, wqkv_ref, wout_ref, bias_hbm, gain_hbm, out_ref,
    tok_ref, bias_ref, gain_ref, wqkv, wout, regrouped, halo_out, main_in, halo_in, bias_full, qkv, returned,
    weight_sems, main_send, main_recv, halo_send, halo_recv, back_send, back_recv,
):
    kernel, heads = bias_ref.shape[0], bias_ref.shape[3]
    rows, x_cells, width = tok_ref.shape[2:]
    chunk = x_cells // ring
    y_total = rows * ring
    head_dim = width // heads
    lanes = y_total * chunk
    groups = width // lanes
    per_group = lanes // head_dim
    halo_rows, half_width = halo_in.shape[1:]
    halo_slots = 2 * radius
    halo_cells = rows * halo_slots
    halo_keys = ring * halo_cells
    keys = 3 * lanes
    gz, gy = lax.axis_index("gz"), lax.axis_index("gy")
    mine, base = gz // half, gz % half
    slot = mine * ring + gy
    partners = [(dm, dg) for dm in reversed(range(members)) for dg in range(ring) if (dm, dg) != (0, 0)]

    def member(dm):
        return lax.rem(mine + dm, members)

    def ring_place(dg):
        return lax.rem(gy + dg, ring)

    def target(dm, dg):
        return (base + member(dm) * half, ring_place(dg))

    barrier = pltpu.get_barrier_semaphore()
    for dm, dg in partners:
        pl.semaphore_signal(barrier, inc=1, device_id=target(dm, dg), device_id_type=MESH_IDS)
    load_tokens = pltpu.make_async_copy(tok_hbm, tok_ref, weight_sems.at[2])
    load_bias = pltpu.make_async_copy(bias_hbm, bias_ref, weight_sems.at[3])
    load_gain = pltpu.make_async_copy(gain_hbm, gain_ref, weight_sems.at[4])
    load_tokens.start()
    load_bias.start()
    load_qkv = pltpu.make_async_copy(wqkv_ref, wqkv, weight_sems.at[0])
    load_out = pltpu.make_async_copy(wout_ref, wout, weight_sems.at[1])
    load_qkv.start()
    load_out.start()
    load_gain.start()

    pl.semaphore_wait(barrier, len(partners))
    sends = []
    for dm, dg in partners:
        index = dm * ring + dg
        columns = pl.ds(pl.multiple_of(ring_place(dg) * chunk, chunk), chunk)
        sends.append(
            pltpu.make_async_remote_copy(
                src_ref=tok_hbm.at[0, member(dm), :, columns, :],
                dst_ref=main_in.at[slot],
                send_sem=main_send.at[index],
                recv_sem=main_recv.at[index],
                device_id=target(dm, dg),
                device_id_type=MESH_IDS,
            )
        )
        sends[-1].start()

    count = ring * halo_rows
    line = lax.broadcasted_iota(jnp.int32, (count, rows * x_cells), 0)
    source = lax.broadcasted_iota(jnp.int32, (count, rows * x_cells), 1)
    place, within = line // halo_rows, line % halo_cells
    row, column = within // halo_slots, within % halo_slots
    column_x = place * chunk + jnp.where(column < radius, column - radius, column + chunk - radius)
    wanted = row * x_cells + (column_x + x_cells) % x_cells
    pick = jnp.where(source == wanted, 1.0, 0.0).astype(jnp.bfloat16)
    upper = lax.broadcasted_iota(jnp.int32, (count, half_width), 0) % halo_rows < halo_cells
    load_tokens.wait()
    for plane in range(members):
        flat = tok_ref[0, plane].reshape(rows * x_cells, width)
        picked = jnp.dot(pick, flat, preferred_element_type=jnp.float32)
        folded = jnp.where(upper, picked[:, :half_width], picked[:, half_width:])
        halo_out[plane] = folded.astype(jnp.bfloat16).reshape(ring, halo_rows, half_width)

    for dm, dg in partners:
        index = dm * ring + dg
        sends.append(
            pltpu.make_async_remote_copy(
                src_ref=halo_out.at[member(dm), ring_place(dg)],
                dst_ref=halo_in.at[slot],
                send_sem=halo_send.at[index],
                recv_sem=halo_recv.at[index],
                device_id=target(dm, dg),
                device_id_type=MESH_IDS,
            )
        )
        sends[-1].start()
    own_columns = pl.ds(pl.multiple_of(gy * chunk, chunk), chunk)
    main_in[slot] = tok_ref[0, mine, :, own_columns, :]
    halo_in[slot] = halo_out[mine, gy]

    x_query = lax.broadcasted_iota(jnp.int32, (chunk, lanes), 0)
    lane = lax.broadcasted_iota(jnp.int32, (chunk, lanes), 1)

    def tap_map(y_key, x_key, valid):
        tap_y = (y_key + radius) % y_total
        tap_x = x_key - x_query + radius
        inside = valid & (tap_y < kernel) & (tap_x >= 0) & (tap_x < kernel)
        return jnp.where(inside, tap_y * kernel + tap_x, -1)

    main_taps = tap_map(lane // chunk, lane % chunk, lane >= 0)
    halo_lane = lane % (y_total * halo_slots)
    halo_column = halo_lane % halo_slots
    halo_x = jnp.where(halo_column < radius, halo_column - radius, halo_column + chunk - radius)
    halo_taps = tap_map(halo_lane // halo_slots, halo_x, lane >= 0)
    halo_plane = lane // halo_keys

    load_bias.wait()
    merged_bias = []
    for taps in tap_groups:
        parts = [bias_ref[i] for i in taps]
        top = functools.reduce(jnp.maximum, parts)
        merged_bias.append((top + jnp.log(sum(jnp.exp(part - top) for part in parts))) * LOG2E)
    head_lane = lax.broadcasted_iota(jnp.int32, (kernel, kernel, heads), 2)

    def bias_of_head(head, carry):
        mains, halos = [], []
        for merged in merged_bias:
            column = jnp.sum(jnp.where(head_lane == head, merged, 0.0), axis=2, keepdims=True)
            spread = jnp.broadcast_to(column, (kernel, kernel, lanes))
            main = jnp.full((chunk, lanes), MASKED, jnp.float32)
            halo = main
            for tap_y in range(kernel):
                for tap_x in range(kernel):
                    value = spread[tap_y, tap_x : tap_x + 1, :]
                    main = jnp.where(main_taps == tap_y * kernel + tap_x, value, main)
                    halo = jnp.where(halo_taps == tap_y * kernel + tap_x, value, halo)
            mains.append(main)
            halos.append(halo)
        for y in range(y_total):
            here = pl.ds(y * chunk, chunk)
            turned = [pltpu.roll(main, y * chunk, 1) if y else main for main in mains]
            turned_halo = [pltpu.roll(halo, y * halo_slots, 1) if y else halo for halo in halos]
            for plane in range(2):
                bias_full[head, plane, here, 0:lanes] = turned[plane]
                bias_full[head, plane, here, lanes : 2 * lanes] = turned[1 - plane]
                bias_full[head, plane, here, 2 * lanes : 3 * lanes] = jnp.where(
                    halo_plane == 0,
                    turned_halo[plane],
                    jnp.where(halo_plane == 1, turned_halo[1 - plane], MASKED),
                )
        return carry

    lax.fori_loop(0, heads, bias_of_head, 0)

    span = 3 * lanes
    before = lax.broadcasted_iota(jnp.int32, (span, span), 0)
    after = lax.broadcasted_iota(jnp.int32, (span, span), 1)
    origin = (after % lanes) // head_dim * (3 * head_dim) + after // lanes * head_dim + after % head_dim
    order = jnp.where(before == origin, 1.0, 0.0).astype(jnp.bfloat16)
    load_qkv.wait()
    for group in range(groups):
        regrouped[group] = jnp.dot(
            wqkv[:, group * span : (group + 1) * span], order, preferred_element_type=jnp.float32
        ).astype(jnp.bfloat16)

    def project(dm):
        for copy, (sent_dm, _) in zip(sends, partners + partners):
            if sent_dm == dm:
                copy.wait_recv()
        plane = member(dm)
        slots = pl.ds(plane * ring, ring)
        main_rows = pl.ds(pl.multiple_of(plane * lanes, lanes), lanes)
        halo_keys_at = pl.ds(pl.multiple_of(members * lanes + plane * halo_keys, halo_keys), halo_keys)
        main = main_in[slots].reshape(lanes, width)
        folded = halo_in[slots].reshape(ring * halo_rows, half_width)
        for group in range(groups):
            weight = regrouped[group]
            qkv[group, main_rows] = jnp.dot(
                main, weight, preferred_element_type=jnp.float32
            ).astype(jnp.bfloat16)
            first = jnp.dot(folded, weight[:half_width], preferred_element_type=jnp.float32)
            second = jnp.dot(folded, weight[half_width:], preferred_element_type=jnp.float32)
            both = (
                first.reshape(ring, halo_rows, span)[:, :halo_cells]
                + second.reshape(ring, halo_rows, span)[:, halo_cells:]
            )
            qkv[group, halo_keys_at] = both.reshape(halo_keys, span).astype(jnp.bfloat16)

    unused = keys - members * (lanes + halo_keys)
    for group in range(groups):
        qkv[group, keys - unused : keys] = jnp.zeros((unused, span), jnp.bfloat16)
    for dm in range(members):
        project(dm)

    block = lanes // SPLITS
    places = ring // SPLITS
    owner = lax.broadcasted_iota(jnp.int32, (block, lanes), 1) // head_dim
    ones = jnp.ones((keys, lanes), jnp.bfloat16)
    load_out.wait()
    load_gain.wait()
    backs = []
    landing = out_ref.at[0, mine, :, own_columns, :]
    for dm, part in [(dm, part) for dm in reversed(range(members)) for part in range(SPLITS)]:
        plane = member(dm)
        first_row = part * block
        query_rows = pl.ds(pl.multiple_of(plane * lanes + first_row, block), block)

        def attend(group):
            query = qkv[group, query_rows, 0:lanes]
            key = qkv[group, :, lanes : 2 * lanes]
            value = jnp.concatenate([qkv[group, :, 2 * lanes : 3 * lanes], ones], axis=1)
            own = jnp.concatenate(
                [jnp.where(owner == within, query, jnp.zeros_like(query)) for within in range(per_group)], axis=0
            )
            scores = lax.dot_general(
                own, key, (((1,), (1,)), ((), ())), preferred_element_type=jnp.float32
            )
            bias = bias_full[
                group * per_group : (group + 1) * per_group, plane, first_row : first_row + block
            ]
            scores = scores * (scale * LOG2E) + bias.reshape(per_group * block, keys)
            row_max = jnp.max(scores, axis=1, keepdims=True)
            weights = jnp.exp2(scores - row_max).astype(jnp.bfloat16)
            both = jnp.dot(weights, value, preferred_element_type=jnp.float32)
            both = both.reshape(per_group, block, 2 * lanes)
            mixed, total = both[0, :, :lanes], both[0, :, lanes:]
            for within in range(1, per_group):
                mixed = jnp.where(owner == within, both[within, :, :lanes], mixed)
                total = jnp.where(owner == within, both[within, :, lanes:], total)
            return (mixed / total).astype(jnp.bfloat16)

        joined = jnp.concatenate([attend(group) for group in range(groups)], axis=1)
        projection = jnp.dot(joined, wout[...], preferred_element_type=jnp.float32)
        mean_sq = jnp.mean(projection * projection, axis=-1, keepdims=True)
        update = (projection * lax.rsqrt(mean_sq + 1e-06) * gain_ref[...]).astype(jnp.bfloat16)
        finished = update.reshape(places, rows, chunk, width)
        returned[dm, part * places : (part + 1) * places] = finished
        for place in range(part * places, (part + 1) * places):
            going = returned.at[dm, place]
            if dm == 0:
                @pl.when(place == gy)
                def _():
                    out_ref[0, mine, :, own_columns, :] = returned[dm, place]

                @pl.when(place != gy)
                def _():
                    pltpu.make_async_remote_copy(
                        src_ref=going, dst_ref=landing,
                        send_sem=back_send.at[place], recv_sem=back_recv.at[gy],
                        device_id=(gz, place), device_id_type=MESH_IDS,
                    ).start()
            else:
                back = pltpu.make_async_remote_copy(
                    src_ref=going, dst_ref=landing,
                    send_sem=back_send.at[ring + place], recv_sem=back_recv.at[ring + gy],
                    device_id=(base + plane * half, place), device_id_type=MESH_IDS,
                )
                back.start()
    for copy in sends:
        copy.wait_send()
    for dm in reversed(range(members)):
        for place in range(ring):
            def finish():
                pltpu.make_async_remote_copy(
                    src_ref=returned.at[dm, place], dst_ref=landing,
                    send_sem=back_send.at[dm * ring + place], recv_sem=back_recv.at[dm * ring + place],
                    device_id=(base + member(dm) * half, place), device_id_type=MESH_IDS,
                ).wait()

            if dm:
                finish()
            else:
                pl.when(place != gy)(finish)


def pair_plan(mesh_shape, depth_total, shapes):
    boxes, planes, rows, x_cells, width, heads, kernel = shapes
    depth_devices, ring = mesh_shape
    radius = kernel // 2
    head_dim = width // heads
    offsets = [DILATION_DEPTH * (i - radius) % depth_total for i in range(kernel)]
    halo_slots = 2 * radius
    if boxes != 1 or planes != 2 or depth_total != 2 * DILATION_DEPTH or depth_devices % 2:
        return None
    if x_cells % ring or kernel % 2 == 0:
        return None
    chunk, y_total = x_cells // ring, rows * ring
    lanes = chunk * y_total
    if lanes != 128 or chunk % 16 or kernel > y_total or 2 * y_total * halo_slots > lanes:
        return None
    if rows * halo_slots != 8 or lanes % head_dim or width % (2 * lanes) or ring % SPLITS:
        return None
    return halo_slots, [[i for i in range(kernel) if offsets[i] == p * DILATION_DEPTH] for p in range(2)]


def fused(plan, depth_devices, ring, tokens, w_qkv, w_out, rel_bias, gain):
    halo_slots, tap_groups = plan
    _, planes, rows, x_cells, width = tokens.shape
    heads, kernel = rel_bias.shape[0], rel_bias.shape[1]
    chunk = x_cells // ring
    lanes = chunk * rows * ring
    groups = width // lanes
    halo_rows = 2 * rows * halo_slots
    members, slots = planes, planes * ring
    keys = 3 * lanes
    vmem = pl.BlockSpec(memory_space=pltpu.VMEM)
    hbm = pl.BlockSpec(memory_space=pltpu.HBM)
    body_of = functools.partial(
        kernel_body, members, ring, depth_devices // 2, tap_groups, kernel // 2,
        float(width // heads) ** (-0.5),
    )
    dma = pltpu.SemaphoreType.DMA
    return pl.pallas_call(
        body_of,
        out_shape=jax.ShapeDtypeStruct(tokens.shape, jnp.bfloat16),
        in_specs=[hbm] * 5,
        out_specs=vmem,
        scratch_shapes=[
            pltpu.VMEM(tokens.shape, jnp.bfloat16),
            pltpu.VMEM(rel_bias.shape[1:] + (heads,), jnp.float32),
            pltpu.VMEM((1, width), jnp.float32),
            pltpu.VMEM(w_qkv.shape, jnp.bfloat16),
            pltpu.VMEM(w_out.shape, jnp.bfloat16),
            pltpu.VMEM((groups, width, 3 * lanes), jnp.bfloat16),
            pltpu.VMEM((members, ring, halo_rows, width // 2), jnp.bfloat16),
            pltpu.VMEM((slots, rows, chunk, width), jnp.bfloat16),
            pltpu.VMEM((slots, halo_rows, width // 2), jnp.bfloat16),
            pltpu.VMEM((heads, members, lanes, keys), jnp.float32),
            pltpu.VMEM((groups, keys, 3 * lanes), jnp.bfloat16),
            pltpu.VMEM((members, ring, rows, chunk, width), jnp.bfloat16),
            dma((5,)), dma((slots,)), dma((slots,)), dma((slots,)), dma((slots,)),
            dma((slots,)), dma((slots,)),
        ],
        compiler_params=pltpu.CompilerParams(
            collective_id=0, has_side_effects=True, vmem_limit_bytes=62 * 1024 * 1024
        ),
    )(tokens, w_qkv, w_out, jnp.transpose(rel_bias, (1, 2, 3, 0)), gain.reshape(1, width))


def solution(mesh):
    depth_devices, ring = mesh.shape["gz"], mesh.shape["gy"]

    def chosen(tokens, w_qkv, w_out, rel_bias, gain):
        shapes = tokens.shape + rel_bias.shape[:2]
        plan = pair_plan((depth_devices, ring), tokens.shape[1] * depth_devices, shapes)
        if plan is None:
            return body(tokens, w_qkv, w_out, rel_bias, gain)
        return fused(plan, depth_devices, ring, tokens, w_qkv, w_out, rel_bias, gain)

    in_specs = (P(None, "gz", "gy", None, None), P(), P(), P(), P())
    out_specs = P(None, "gz", "gy", None, None)
    return jax.shard_map(chosen, mesh=mesh, in_specs=in_specs, out_specs=out_specs, check_vma=False)
```

```python
import functools

import jax
import jax.numpy as jnp
from jax import lax
from jax.experimental import pallas as pl
from jax.experimental.pallas import tpu as pltpu
from jax.sharding import PartitionSpec as P

DILATION_DEPTH = 8


def shifted(block, axis, distance):
    devices = range(lax.axis_size(axis))
    route = [((i - distance) % len(devices), i) for i in devices]
    return lax.ppermute(block, axis, route)


def pick_rows(y_rows, per_row):
    chosen = 1
    for candidate in range(1, y_rows + 1):
        if y_rows % candidate == 0 and candidate * per_row <= 1024:
            chosen = candidate
    return chosen


def collect_planes(key_value, depth_stride, kernel_radius):
    axis_count = lax.axis_size("gz")
    received = {0: key_value}
    for offset in range(-kernel_radius, kernel_radius + 1):
        if offset != 0:
            distance = -offset * depth_stride % axis_count
            if distance == 0:
                received[offset] = key_value
            else:
                received[offset] = shifted(key_value, "gz", distance)
    return jnp.stack([received[offset] for offset in range(-kernel_radius, kernel_radius + 1)], 0)


def neighbourhood(queries, padded, bias_part):
    boxes, depth_planes, y_rows, x_cells, local_heads, head_dim = queries.shape
    kernel = padded.shape[0]
    kernel_radius = kernel // 2
    score_scale = float(head_dim) ** (-0.5)
    block_rows = pick_rows(y_rows, local_heads * x_cells)
    row_blocks = y_rows // block_rows
    block_count = boxes * depth_planes * row_blocks

    def tap_window(wide, tap_y):
        rows_part = wide[:, tap_y : tap_y + block_rows]
        return jnp.stack([rows_part[:, :, tap_x : tap_x + x_cells] for tap_x in range(kernel)], 1)

    def one_block(block_index):
        slab_index = block_index // row_blocks
        row_start = block_index % row_blocks * block_rows
        box_index = slab_index // depth_planes
        depth_plane_index = slab_index % depth_planes
        query_block = lax.dynamic_slice(
            queries,
            (box_index, depth_plane_index, row_start, 0, 0, 0),
            (1, 1, block_rows, x_cells, local_heads, head_dim),
        )[0, 0]
        pair_block = lax.dynamic_slice(
            padded,
            (0, box_index, depth_plane_index, row_start, 0, 0, 0, 0),
            (kernel, 1, 1, block_rows + 2 * kernel_radius, x_cells, local_heads, 2, head_dim),
        )[:, 0, 0]
        wide = jnp.concatenate(
            [
                pair_block[:, :, x_cells - kernel_radius :],
                pair_block,
                pair_block[:, :, :kernel_radius],
            ],
            axis=2,
        )
        score_parts = []
        for tap_y in range(kernel):
            window = tap_window(wide, tap_y)
            score_parts.append(
                jnp.einsum(
                    "yxhd,abyxhd->yhxab",
                    query_block,
                    window[..., 0, :],
                    preferred_element_type=jnp.float32,
                )
            )
        scores = jnp.stack(score_parts, 4) * score_scale + bias_part[None, :, None]
        row_max = jnp.max(scores, axis=(3, 4, 5), keepdims=True)
        exponent = jnp.exp(scores - row_max)
        weights = (exponent / jnp.sum(exponent, axis=(3, 4, 5), keepdims=True)).astype(jnp.bfloat16)
        mixed = jnp.zeros((block_rows, x_cells, local_heads, head_dim), jnp.float32)
        for tap_y in range(kernel):
            window = tap_window(wide, tap_y)
            mixed = mixed + jnp.einsum(
                "yhxab,abyxhd->yxhd",
                weights[:, :, :, :, tap_y],
                window[..., 1, :],
                preferred_element_type=jnp.float32,
            )
        return mixed.astype(jnp.bfloat16).reshape(block_rows, x_cells, local_heads * head_dim)

    block_out = lax.map(one_block, jnp.arange(block_count, dtype=jnp.int32))
    return block_out.reshape(boxes, depth_planes, y_rows, x_cells, local_heads * head_dim)


def body(tokens, w_qkv, w_out, rel_bias, gain):
    boxes, depth_planes, y_rows, x_cells, model_width = tokens.shape
    head_count = rel_bias.shape[0]
    kernel = rel_bias.shape[1]
    kernel_radius = kernel // 2
    head_dim = model_width // head_count
    depth_stride = DILATION_DEPTH // depth_planes
    projected = jnp.dot(
        tokens.reshape(-1, model_width), w_qkv, preferred_element_type=jnp.float32
    ).astype(jnp.bfloat16)
    projected = projected.reshape(boxes, depth_planes, y_rows, x_cells, 3 * model_width)
    exchanged = lax.all_to_all(projected, "gy", split_axis=4, concat_axis=2, tiled=True)
    local_heads = exchanged.shape[-1] // (3 * head_dim)
    unpacked = exchanged.reshape(exchanged.shape[:4] + (local_heads, 3, head_dim))
    queries = unpacked[..., 0, :]
    key_value = unpacked[..., 1:, :]
    plane_taps = collect_planes(key_value, depth_stride, kernel_radius)
    padded = jnp.concatenate(
        [plane_taps[:, :, :, -kernel_radius:], plane_taps, plane_taps[:, :, :, :kernel_radius]],
        axis=3,
    )
    head_start = lax.axis_index("gy") * local_heads
    bias_part = lax.dynamic_slice_in_dim(rel_bias, head_start, local_heads, 0)
    gathered = neighbourhood(queries, padded, bias_part)
    attended = lax.all_to_all(gathered, "gy", split_axis=2, concat_axis=4, tiled=True)
    projection = jnp.dot(
        attended.reshape(-1, model_width), w_out, preferred_element_type=jnp.float32
    )
    mean_sq = jnp.mean(projection * projection, axis=-1, keepdims=True)
    update = (projection * lax.rsqrt(mean_sq + 1e-06) * gain).astype(jnp.bfloat16)
    return update.reshape(boxes, depth_planes, y_rows, x_cells, model_width)


SPLITS = 1
MASKED = -1e30
LOG2E = 1.4426950408889634
MESH_IDS = pl.DeviceIdType.MESH


def kernel_body(
    members, ring, half, tap_groups, radius, scale,
    tok_hbm, wqkv_ref, wout_ref, bias_hbm, gain_hbm, out_ref,
    tok_ref, bias_ref, gain_ref, wqkv, wout, regrouped, halo_out, main_in, halo_in, bias_full, qkv, returned,
    weight_sems, main_send, main_recv, halo_send, halo_recv, back_send, back_recv, local_sem,
):
    kernel, heads = bias_ref.shape[0], bias_ref.shape[3]
    rows, x_cells, width = tok_ref.shape[2:]
    chunk = x_cells // ring
    y_total = rows * ring
    head_dim = width // heads
    lanes = y_total * chunk
    groups = width // lanes
    per_group = lanes // head_dim
    halo_rows, half_width = halo_in.shape[1:]
    halo_slots = 2 * radius
    halo_cells = rows * halo_slots
    halo_keys = ring * halo_cells
    keys = 3 * lanes
    gz, gy = lax.axis_index("gz"), lax.axis_index("gy")
    mine, base = gz // half, gz % half
    slot = mine * ring + gy
    partners = [(dm, dg) for dm in reversed(range(members)) for dg in range(ring) if (dm, dg) != (0, 0)]

    def member(dm):
        return lax.rem(mine + dm, members)

    def ring_place(dg):
        return lax.rem(gy + dg, ring)

    def target(dm, dg):
        return (base + member(dm) * half, ring_place(dg))

    barrier = pltpu.get_barrier_semaphore()
    for dm, dg in partners:
        pl.semaphore_signal(barrier, inc=1, device_id=target(dm, dg), device_id_type=MESH_IDS)
    load_tokens = pltpu.make_async_copy(tok_hbm, tok_ref, weight_sems.at[2])
    load_bias = pltpu.make_async_copy(bias_hbm, bias_ref, weight_sems.at[3])
    load_gain = pltpu.make_async_copy(gain_hbm, gain_ref, weight_sems.at[4])
    load_tokens.start()
    load_bias.start()
    load_qkv = pltpu.make_async_copy(wqkv_ref, wqkv, weight_sems.at[0])
    load_out = pltpu.make_async_copy(wout_ref, wout, weight_sems.at[1])
    load_qkv.start()
    load_out.start()
    load_gain.start()

    pl.semaphore_wait(barrier, len(partners))
    sends = []
    for dm, dg in partners:
        index = dm * ring + dg
        columns = pl.ds(pl.multiple_of(ring_place(dg) * chunk, chunk), chunk)
        sends.append(
            pltpu.make_async_remote_copy(
                src_ref=tok_hbm.at[0, member(dm), :, columns, :],
                dst_ref=main_in.at[slot],
                send_sem=main_send.at[index],
                recv_sem=main_recv.at[index],
                device_id=target(dm, dg),
                device_id_type=MESH_IDS,
            )
        )
        sends[-1].start()

    count = ring * halo_rows
    line = lax.broadcasted_iota(jnp.int32, (count, rows * x_cells), 0)
    source = lax.broadcasted_iota(jnp.int32, (count, rows * x_cells), 1)
    place, within = line // halo_rows, line % halo_cells
    row, column = within // halo_slots, within % halo_slots
    column_x = place * chunk + jnp.where(column < radius, column - radius, column + chunk - radius)
    wanted = row * x_cells + (column_x + x_cells) % x_cells
    pick = jnp.where(source == wanted, 1.0, 0.0).astype(jnp.bfloat16)
    upper = lax.broadcasted_iota(jnp.int32, (count, half_width), 0) % halo_rows < halo_cells
    load_tokens.wait()
    for plane in range(members):
        flat = tok_ref[0, plane].reshape(rows * x_cells, width)
        picked = jnp.dot(pick, flat, preferred_element_type=jnp.float32)
        folded = jnp.where(upper, picked[:, :half_width], picked[:, half_width:])
        halo_out[plane] = folded.astype(jnp.bfloat16).reshape(ring, halo_rows, half_width)

    for dm, dg in partners:
        index = dm * ring + dg
        sends.append(
            pltpu.make_async_remote_copy(
                src_ref=halo_out.at[member(dm), ring_place(dg)],
                dst_ref=halo_in.at[slot],
                send_sem=halo_send.at[index],
                recv_sem=halo_recv.at[index],
                device_id=target(dm, dg),
                device_id_type=MESH_IDS,
            )
        )
        sends[-1].start()
    own_columns = pl.ds(pl.multiple_of(gy * chunk, chunk), chunk)
    main_in[slot] = tok_ref[0, mine, :, own_columns, :]
    halo_in[slot] = halo_out[mine, gy]

    x_query = lax.broadcasted_iota(jnp.int32, (chunk, lanes), 0)
    lane = lax.broadcasted_iota(jnp.int32, (chunk, lanes), 1)

    def tap_map(y_key, x_key, valid):
        tap_y = (y_key + radius) % y_total
        tap_x = x_key - x_query + radius
        inside = valid & (tap_y < kernel) & (tap_x >= 0) & (tap_x < kernel)
        return jnp.where(inside, tap_y * kernel + tap_x, -1)

    main_taps = tap_map(lane // chunk, lane % chunk, lane >= 0)
    halo_lane = lane % (y_total * halo_slots)
    halo_column = halo_lane % halo_slots
    halo_x = jnp.where(halo_column < radius, halo_column - radius, halo_column + chunk - radius)
    halo_taps = tap_map(halo_lane // halo_slots, halo_x, lane >= 0)
    halo_plane = lane // halo_keys

    load_bias.wait()
    merged_bias = []
    for taps in tap_groups:
        parts = [bias_ref[i] for i in taps]
        top = functools.reduce(jnp.maximum, parts)
        merged_bias.append((top + jnp.log(sum(jnp.exp(part - top) for part in parts))) * LOG2E)
    head_lane = lax.broadcasted_iota(jnp.int32, (kernel, kernel, heads), 2)

    def bias_of_head(head, carry):
        mains, halos = [], []
        for merged in merged_bias:
            column = jnp.sum(jnp.where(head_lane == head, merged, 0.0), axis=2, keepdims=True)
            spread = jnp.broadcast_to(column, (kernel, kernel, lanes))
            main = jnp.full((chunk, lanes), MASKED, jnp.float32)
            halo = main
            for tap_y in range(kernel):
                for tap_x in range(kernel):
                    value = spread[tap_y, tap_x : tap_x + 1, :]
                    main = jnp.where(main_taps == tap_y * kernel + tap_x, value, main)
                    halo = jnp.where(halo_taps == tap_y * kernel + tap_x, value, halo)
            mains.append(main)
            halos.append(halo)
        for y in range(y_total):
            here = pl.ds(y * chunk, chunk)
            turned = [pltpu.roll(main, y * chunk, 1) if y else main for main in mains]
            turned_halo = [pltpu.roll(halo, y * halo_slots, 1) if y else halo for halo in halos]
            for plane in range(2):
                bias_full[head, plane, here, 0:lanes] = turned[plane]
                bias_full[head, plane, here, lanes : 2 * lanes] = turned[1 - plane]
                bias_full[head, plane, here, 2 * lanes : 3 * lanes] = jnp.where(
                    halo_plane == 0,
                    turned_halo[plane],
                    jnp.where(halo_plane == 1, turned_halo[1 - plane], MASKED),
                )
        return carry

    lax.fori_loop(0, heads, bias_of_head, 0)

    span = 3 * lanes
    before = lax.broadcasted_iota(jnp.int32, (span, span), 0)
    after = lax.broadcasted_iota(jnp.int32, (span, span), 1)
    origin = (after % lanes) // head_dim * (3 * head_dim) + after // lanes * head_dim + after % head_dim
    order = jnp.where(before == origin, 1.0, 0.0).astype(jnp.bfloat16)
    load_qkv.wait()
    for group in range(groups):
        regrouped[group] = jnp.dot(
            wqkv[:, group * span : (group + 1) * span], order, preferred_element_type=jnp.float32
        ).astype(jnp.bfloat16)

    def project(dm):
        for copy, (sent_dm, _) in zip(sends, partners + partners):
            if sent_dm == dm:
                copy.wait_recv()
        plane = member(dm)
        slots = pl.ds(plane * ring, ring)
        main_rows = pl.ds(pl.multiple_of(plane * lanes, lanes), lanes)
        halo_keys_at = pl.ds(pl.multiple_of(members * lanes + plane * halo_keys, halo_keys), halo_keys)
        main = main_in[slots].reshape(lanes, width)
        folded = halo_in[slots].reshape(ring * halo_rows, half_width)
        for group in range(groups):
            weight = regrouped[group]
            qkv[group, main_rows] = jnp.dot(
                main, weight, preferred_element_type=jnp.float32
            ).astype(jnp.bfloat16)
            first = jnp.dot(folded, weight[:half_width], preferred_element_type=jnp.float32)
            second = jnp.dot(folded, weight[half_width:], preferred_element_type=jnp.float32)
            both = (
                first.reshape(ring, halo_rows, span)[:, :halo_cells]
                + second.reshape(ring, halo_rows, span)[:, halo_cells:]
            )
            qkv[group, halo_keys_at] = both.reshape(halo_keys, span).astype(jnp.bfloat16)

    unused = keys - members * (lanes + halo_keys)
    for group in range(groups):
        qkv[group, keys - unused : keys] = jnp.zeros((unused, span), jnp.bfloat16)
    for dm in range(members):
        project(dm)

    block = lanes // SPLITS
    places = ring // SPLITS
    owner = lax.broadcasted_iota(jnp.int32, (block, lanes), 1) // head_dim
    ones = jnp.ones((keys, lanes), jnp.bfloat16)
    load_out.wait()
    load_gain.wait()
    backs = []
    landing = out_ref.at[0, mine, :, own_columns, :]
    for dm, part in [(dm, part) for dm in reversed(range(members)) for part in range(SPLITS)]:
        plane = member(dm)
        first_row = part * block
        query_rows = pl.ds(pl.multiple_of(plane * lanes + first_row, block), block)

        def attend(group):
            query = qkv[group, query_rows, 0:lanes]
            key = qkv[group, :, lanes : 2 * lanes]
            value = jnp.concatenate([qkv[group, :, 2 * lanes : 3 * lanes], ones], axis=1)
            own = jnp.concatenate(
                [jnp.where(owner == within, query, jnp.zeros_like(query)) for within in range(per_group)], axis=0
            )
            scores = lax.dot_general(
                own, key, (((1,), (1,)), ((), ())), preferred_element_type=jnp.float32
            )
            bias = bias_full[
                group * per_group : (group + 1) * per_group, plane, first_row : first_row + block
            ]
            scores = scores * (scale * LOG2E) + bias.reshape(per_group * block, keys)
            row_max = jnp.max(scores, axis=1, keepdims=True)
            weights = jnp.exp2(scores - row_max).astype(jnp.bfloat16)
            both = jnp.dot(weights, value, preferred_element_type=jnp.float32)
            both = both.reshape(per_group, block, 2 * lanes)
            mixed, total = both[0, :, :lanes], both[0, :, lanes:]
            for within in range(1, per_group):
                mixed = jnp.where(owner == within, both[within, :, :lanes], mixed)
                total = jnp.where(owner == within, both[within, :, lanes:], total)
            return (mixed / total).astype(jnp.bfloat16)

        joined = jnp.concatenate([attend(group) for group in range(groups)], axis=1)
        projection = jnp.dot(joined, wout[...], preferred_element_type=jnp.float32)
        mean_sq = jnp.mean(projection * projection, axis=-1, keepdims=True)
        update = (projection * lax.rsqrt(mean_sq + 1e-06) * gain_ref[...]).astype(jnp.bfloat16)
        finished = update.reshape(places, rows, chunk, width)
        returned[dm, part * places : (part + 1) * places] = finished
        for place in range(part * places, (part + 1) * places):
            going = returned.at[dm, place]
            if dm == 0:
                @pl.when(place == gy)
                def _():
                    pltpu.make_async_copy(going, landing, local_sem).start()

                @pl.when(place != gy)
                def _():
                    pltpu.make_async_remote_copy(
                        src_ref=going, dst_ref=landing,
                        send_sem=back_send.at[place], recv_sem=back_recv.at[gy],
                        device_id=(gz, place), device_id_type=MESH_IDS,
                    ).start()
            else:
                back = pltpu.make_async_remote_copy(
                    src_ref=going, dst_ref=landing,
                    send_sem=back_send.at[ring + place], recv_sem=back_recv.at[ring + gy],
                    device_id=(base + plane * half, place), device_id_type=MESH_IDS,
                )
                back.start()
    for copy in sends:
        copy.wait_send()
    for dm in reversed(range(members)):
        for place in range(ring):
            def finish():
                pltpu.make_async_remote_copy(
                    src_ref=returned.at[dm, place], dst_ref=landing,
                    send_sem=back_send.at[dm * ring + place], recv_sem=back_recv.at[dm * ring + place],
                    device_id=(base + member(dm) * half, place), device_id_type=MESH_IDS,
                ).wait()

            if dm:
                finish()
            else:
                pl.when(place != gy)(finish)

                @pl.when(place == gy)
                def _():
                    pltpu.make_async_copy(returned.at[dm, place], landing, local_sem).wait()


def pair_plan(mesh_shape, depth_total, shapes):
    boxes, planes, rows, x_cells, width, heads, kernel = shapes
    depth_devices, ring = mesh_shape
    radius = kernel // 2
    head_dim = width // heads
    offsets = [DILATION_DEPTH * (i - radius) % depth_total for i in range(kernel)]
    halo_slots = 2 * radius
    if boxes != 1 or planes != 2 or depth_total != 2 * DILATION_DEPTH or depth_devices % 2:
        return None
    if x_cells % ring or kernel % 2 == 0:
        return None
    chunk, y_total = x_cells // ring, rows * ring
    lanes = chunk * y_total
    if lanes != 128 or chunk % 16 or kernel > y_total or 2 * y_total * halo_slots > lanes:
        return None
    if rows * halo_slots != 8 or lanes % head_dim or width % (2 * lanes) or ring % SPLITS:
        return None
    return halo_slots, [[i for i in range(kernel) if offsets[i] == p * DILATION_DEPTH] for p in range(2)]


def fused(plan, depth_devices, ring, tokens, w_qkv, w_out, rel_bias, gain):
    halo_slots, tap_groups = plan
    _, planes, rows, x_cells, width = tokens.shape
    heads, kernel = rel_bias.shape[0], rel_bias.shape[1]
    chunk = x_cells // ring
    lanes = chunk * rows * ring
    groups = width // lanes
    halo_rows = 2 * rows * halo_slots
    members, slots = planes, planes * ring
    keys = 3 * lanes
    hbm = pl.BlockSpec(memory_space=pltpu.HBM)
    body_of = functools.partial(
        kernel_body, members, ring, depth_devices // 2, tap_groups, kernel // 2,
        float(width // heads) ** (-0.5),
    )
    dma = pltpu.SemaphoreType.DMA
    return pl.pallas_call(
        body_of,
        out_shape=jax.ShapeDtypeStruct(tokens.shape, jnp.bfloat16),
        in_specs=[hbm] * 5,
        out_specs=hbm,
        scratch_shapes=[
            pltpu.VMEM(tokens.shape, jnp.bfloat16),
            pltpu.VMEM(rel_bias.shape[1:] + (heads,), jnp.float32),
            pltpu.VMEM((1, width), jnp.float32),
            pltpu.VMEM(w_qkv.shape, jnp.bfloat16),
            pltpu.VMEM(w_out.shape, jnp.bfloat16),
            pltpu.VMEM((groups, width, 3 * lanes), jnp.bfloat16),
            pltpu.VMEM((members, ring, halo_rows, width // 2), jnp.bfloat16),
            pltpu.VMEM((slots, rows, chunk, width), jnp.bfloat16),
            pltpu.VMEM((slots, halo_rows, width // 2), jnp.bfloat16),
            pltpu.VMEM((heads, members, lanes, keys), jnp.float32),
            pltpu.VMEM((groups, keys, 3 * lanes), jnp.bfloat16),
            pltpu.VMEM((members, ring, rows, chunk, width), jnp.bfloat16),
            dma((5,)), dma((slots,)), dma((slots,)), dma((slots,)), dma((slots,)),
            dma((slots,)), dma((slots,)), dma,
        ],
        compiler_params=pltpu.CompilerParams(
            collective_id=0, has_side_effects=True, vmem_limit_bytes=62 * 1024 * 1024
        ),
    )(tokens, w_qkv, w_out, jnp.transpose(rel_bias, (1, 2, 3, 0)), gain.reshape(1, width))


def solution(mesh):
    depth_devices, ring = mesh.shape["gz"], mesh.shape["gy"]

    def chosen(tokens, w_qkv, w_out, rel_bias, gain):
        shapes = tokens.shape + rel_bias.shape[:2]
        plan = pair_plan((depth_devices, ring), tokens.shape[1] * depth_devices, shapes)
        if plan is None:
            return body(tokens, w_qkv, w_out, rel_bias, gain)
        return fused(plan, depth_devices, ring, tokens, w_qkv, w_out, rel_bias, gain)

    in_specs = (P(None, "gz", "gy", None, None), P(), P(), P(), P())
    out_specs = P(None, "gz", "gy", None, None)
    return jax.shard_map(chosen, mesh=mesh, in_specs=in_specs, out_specs=out_specs, check_vma=False)
```
